32 devices in a mesh: exp: 8 (over z, core), rep: 4 (over y, x).
Axes of the slice: x: 2, y: 2, z: 4, core: 2. Of those that a mesh axis runs over, the one named last changes fastest.
Arguments:
- tokens: bfloat16 [4096, 1536], P(('exp', 'rep')), may hold values from -6 to 6
- grad_out: bfloat16 [4096, 1536], P(('exp', 'rep')), may hold values from -6 to 6
- expert_ids: int32 [4096, 2], P(('exp', 'rep')), may hold values from 0 to 7, all different within a row; in each aligned block of 128 rows (0 to 127, 128 to 255, ...) at most 40 rows name the same one
- probs: bfloat16 [4096, 2], P(('exp', 'rep')), may hold values from 0.099609375 to 1
- w_gate: bfloat16 [8, 768, 1536], P('exp', 'rep'), may hold values from -0.15625 to 0.15625
- w_up: bfloat16 [8, 768, 1536], P('exp', 'rep'), may hold values from -0.15625 to 0.15625
- w_down: bfloat16 [8, 768, 1536], P('exp', 'rep'), may hold values from -0.21875 to 0.21875
Outputs:
- grad_tokens: bfloat16 [4096, 1536], P(('exp', 'rep'))
- grad_probs: float32 [4096, 2], P(('exp', 'rep'))
- grad_gate: float32 [8, 768, 1536], P('exp', 'rep')
- grad_up: float32 [8, 768, 1536], P('exp', 'rep')
- grad_down: float32 [8, 768, 1536], P('exp', 'rep')
The draws below stay inside these ranges and needn't reach their ends.
Inputs may be any that keep to these rules, and one draw needn't show every extreme that they name: `expert_ids`: each token names two different experts; among the 128 tokens of one device no expert is named more than 40 times, a bound that some block reaches.
All inputs are finite; a program needn't handle non-finite values.
Results may differ from the reference program's by a relative error of at most 0.007.
Values may be sent and summed in bfloat16 or wider, within the bound.
A program may use at most 64 MiB of HBM per device.

```python
import math
import jax
import jax.numpy as jnp
import numpy as np
from jax import lax

D = 1536
H_WIN = 768
TOP = 2
TOK_DEV = 128
EXPERTS = 8
CAP = 40
TOKENS = 4096
N_REP = 4


def block_levels(rng, shape, pieces, low, top_value):
    factor_of, own = 1.0, jax.random.fold_in(rng, 6)
    for position, shards_of in pieces:
        draws = jnp.exp(jax.random.uniform(jax.random.fold_in(own, position), (shards_of,), jnp.float32, low / len(pieces), top_value / len(pieces)))
        factor_of = factor_of * jnp.repeat(draws, shape[position] // shards_of).reshape([-1 if axis == position else 1 for axis in range(len(shape))])
    return factor_of


def deal_out(own_key, own, number, rows, count, top, most, lean):
    sequence = jax.random.permutation(own_key, count)
    crowded, common = load_shares(count, rows * top, most, lean, True), load_shares(count, rows * top, most, lean, False)
    places = jnp.arange(count)

    def named(tallies, offset_by):
        used = int((tallies > 0).sum())
        fixed = max(1, used // 4)
        shifted = fixed + (places - fixed + offset_by * (used - fixed)) % max(1, count - fixed)
        return jnp.zeros((count,), jnp.int32).at[sequence[jnp.where(places < fixed, places, shifted)]].set(jnp.asarray(tallies, jnp.int32))

    tallies = jnp.where(number % 4 == 0, named(crowded, number // 4), named(common, number - number // 4 - 1))
    mixed = jax.random.permutation(jax.random.fold_in(own, 3), count)
    donor, sink = mixed[0:count // 2 * 2:2], mixed[1:count // 2 * 2:2]
    slack = jnp.minimum(tallies[donor] - 1, most - tallies[sink]) // 2
    slack = jnp.where((donor == sequence[0]) | (sink == sequence[0]) | (tallies[sink] == 0), 0, jnp.maximum(slack, 0))
    shifted = jax.random.randint(jax.random.fold_in(own, 4), (count // 2,), 0, 1 << 20) % (slack + 1)
    tallies = tallies.at[donor].add(-shifted).at[sink].add(shifted)
    labels = jnp.searchsorted(jnp.cumsum(tallies), jnp.arange(rows * top), side="right").astype(jnp.int32)
    grid = labels.reshape(top, rows).T
    grid = grid[jax.random.permutation(jax.random.fold_in(own, 1), rows)]
    offset_by = jax.random.randint(jax.random.fold_in(own, 2), (rows, 1), 0, top)
    return jnp.take_along_axis(grid, (jnp.arange(top)[None, :] + offset_by) % top, axis=1)


def load_shares(number_of, total, bound, lean, full):
    weights = [(1 << 20) // math.isqrt(rank ** lean) + 1 for rank in range(1, number_of + 1)]
    largest = bound if full else min(bound, max(-(-total // number_of), total * weights[0] // sum(weights)))
    least = 1 if total - largest >= number_of - 1 else 0
    counts, rest = [largest] + [least] * (number_of - 1), total - largest - least * (number_of - 1)
    while rest > 0:
        free = [i for i in range(1, number_of) if counts[i] < largest] or [i for i in range(1, number_of) if counts[i] < bound]
        whole, left = sum([weights[i] for i in free]), rest
        for i in free:
            extra = min(bound - counts[i], max(1, left * weights[i] // whole), rest)
            counts[i] = counts[i] + extra
            rest = rest - extra
    return np.array(counts)


def bell_draw(rng, dims, scale, most, cuts=(), held_as=jnp.bfloat16):
    entries = scale * jax.random.normal(rng, dims, jnp.float32)
    if cuts:
        entries = entries * block_levels(rng, dims, cuts, -0.22, 0.18)
    return jnp.clip(entries, -most, most).astype(held_as)


def setup_inputs(seed: int = 0) -> dict:
    splits = jax.random.split(jax.random.key(seed), 8)
    tokens = bell_draw(splits[0], (TOKENS, D), 1.0, 6.0, ((0, 32),))
    grad_out = bell_draw(splits[1], (TOKENS, D), 1.0, 6.0, ((0, 32),))
    expert_ids_keys = jax.random.split(jax.random.fold_in(splits[2], 1), TOKENS // TOK_DEV)
    expert_ids_turns = jax.random.permutation(jax.random.fold_in(splits[2], 3), TOKENS // TOK_DEV)
    expert_ids = jax.vmap(lambda own, number: deal_out(jax.random.fold_in(splits[2], 2), own, number, TOK_DEV, EXPERTS, TOP, CAP, 2))(expert_ids_keys, expert_ids_turns).reshape((TOKENS, TOP))
    probs = jnp.clip(0.099609375 + 0.9003906 * jax.random.uniform(splits[3], (TOKENS, TOP), jnp.float32) ** block_levels(splits[3], (TOKENS, TOP), ((0, 32),), -0.2, 0.2), 0.099609375, 1.0).astype(jnp.bfloat16)
    w_gate = bell_draw(splits[4], (EXPERTS, H_WIN, D), D ** -0.5, 0.15625, ((0, 8), (1, 4)))
    w_up = bell_draw(splits[5], (EXPERTS, H_WIN, D), D ** -0.5, 0.15625, ((0, 8), (1, 4)))
    w_down = bell_draw(splits[6], (EXPERTS, H_WIN, D), H_WIN ** -0.5, 0.21875, ((0, 8), (1, 4)))
    return {"tokens": tokens, "grad_out": grad_out, "expert_ids": expert_ids, "probs": probs, "w_gate": w_gate, "w_up": w_up, "w_down": w_down}


def reference(tokens, grad_out, expert_ids, probs, w_gate, w_up, w_down):
    token_total = tokens.shape[0]
    width = tokens.shape[1]
    blocks = token_total // TOK_DEV
    pair_total = 2 * token_total
    flat = expert_ids.reshape(-1).astype(jnp.int32)
    onehot = (flat[:, None] == jnp.arange(EXPERTS, dtype=jnp.int32)[None, :]).astype(jnp.int32)
    running = jnp.cumsum(onehot.reshape(blocks, 2 * TOK_DEV, EXPERTS), axis=1).reshape(pair_total, EXPERTS)
    ranks = jnp.sum((running - 1) * onehot, axis=1).astype(jnp.int32)
    owner = (jnp.arange(pair_total, dtype=jnp.int32) // (2 * TOK_DEV)).astype(jnp.int32)
    slot_of = (owner * CAP + ranks).astype(jnp.int32)
    table = jnp.full((EXPERTS, blocks * CAP), pair_total, dtype=jnp.int32)
    table = table.at[flat, slot_of].set(jnp.arange(pair_total, dtype=jnp.int32))
    token_rows = jnp.concatenate([tokens, jnp.zeros((1, width), tokens.dtype)], axis=0)
    grad_rows = jnp.concatenate([grad_out, jnp.zeros((1, width), grad_out.dtype)], axis=0)
    prob_flat = jnp.concatenate([probs.reshape(-1).astype(jnp.float32), jnp.zeros((1,), jnp.float32)])
    parity = ((jnp.arange(H_WIN, dtype=jnp.int32) // (H_WIN // N_REP)) % 2).astype(jnp.int32)

    def expert_step(carry, inputs):
        pair_grads, prob_grads = carry
        members, gate_w, up_w, down_w = inputs
        source = (members // 2).astype(jnp.int32)
        rows = token_rows[source]
        grads = grad_rows[source]
        weight = prob_flat[members][:, None]
        gate = jnp.dot(rows, gate_w.T, preferred_element_type=jnp.float32)
        up = jnp.dot(rows, up_w.T, preferred_element_type=jnp.float32)
        sig = jax.nn.sigmoid(gate)
        act = gate * sig
        hidden = act * up
        back = jnp.dot(grads, down_w.T, preferred_element_type=jnp.float32)
        d_gate = (weight * back * up * sig * (1.0 + gate * (1.0 - sig))).astype(jnp.bfloat16)
        d_up = (weight * back * act).astype(jnp.bfloat16)
        weighted = (weight * hidden).astype(jnp.bfloat16)
        row_total = jnp.zeros((rows.shape[0], width), jnp.float32)
        prob_total = jnp.zeros((rows.shape[0],), jnp.float32)
        for half in (0, 1):
            select = (parity == half)
            select_b = select.astype(jnp.bfloat16)[None, :]
            part = jnp.dot(d_gate * select_b, gate_w, preferred_element_type=jnp.float32) + jnp.dot(d_up * select_b, up_w, preferred_element_type=jnp.float32)
            part = lax.optimization_barrier(part.astype(jnp.bfloat16)).astype(jnp.float32)
            prob_half = jnp.sum(hidden * back * select.astype(jnp.float32)[None, :], axis=1)
            prob_half = lax.optimization_barrier(prob_half.astype(jnp.bfloat16)).astype(jnp.float32)
            row_total = row_total + part
            prob_total = prob_total + prob_half
        row_total = lax.optimization_barrier(row_total.astype(jnp.bfloat16)).astype(jnp.float32)
        prob_total = lax.optimization_barrier(prob_total.astype(jnp.bfloat16)).astype(jnp.float32)
        grad_g = jnp.dot(d_gate.T, rows, preferred_element_type=jnp.float32)
        grad_u = jnp.dot(d_up.T, rows, preferred_element_type=jnp.float32)
        grad_d = jnp.dot(weighted.T, grads, preferred_element_type=jnp.float32)
        pair_grads = pair_grads.at[members].add(row_total)
        prob_grads = prob_grads.at[members].add(prob_total)
        return (pair_grads, prob_grads), (grad_g, grad_u, grad_d)

    start = (jnp.zeros((pair_total + 1, width), jnp.float32), jnp.zeros((pair_total + 1,), jnp.float32))
    finals, stacked = lax.scan(expert_step, start, (table, w_gate, w_up, w_down))
    pair_grads, prob_grads = finals
    grad_tokens = pair_grads[:pair_total].reshape(token_total, 2, width).sum(axis=1).astype(jnp.bfloat16)
    grad_probs = prob_grads[:pair_total].reshape(token_total, 2)
    return (grad_tokens, grad_probs, stacked[0], stacked[1], stacked[2])
```

```python
import functools

import jax
import jax.numpy as jnp
from jax import lax
from jax.experimental import pallas as pl
from jax.experimental.pallas import tpu as pltpu
from jax.sharding import PartitionSpec as P

F32 = jnp.float32
BF16 = jnp.bfloat16
NT = (((1,), (1,)), ((), ()))
TN = (((0,), (0,)), ((), ()))


def flipped(index, mask, bits):
    for bit in range(bits):
        if mask >> bit & 1:
            index = index + (1 << bit) - 2 * (1 << bit) * (index // (1 << bit) % 2)
    return index


def dot(a, b, dims=(((1,), (0,)), ((), ()))):
    return lax.dot_general(a, b, dims, preferred_element_type=F32)


def layer(
    exp_count,
    rep_count,
    cap,
    select,
    tokens,
    grads,
    w_gate,
    w_up,
    w_down,
    ret,
    ret_prob,
    own_grads,
    peer_grads,
    send,
    recv,
    weights,
    rows,
    row_grads,
    d_gate,
    d_up,
    hid,
    x_send,
    x_recv,
    keep,
    z_send,
    xp_send,
    xp_recv,
    keep_prob,
    zp_send,
    grads_out,
    z_sems,
    x_sems,
    y_sems,
    xr_sems,
    zr_sems,
    xp_sems,
    zp_sems,
    g_sems,
):
    exp_bits = exp_count.bit_length() - 1
    rep_bits = rep_count.bit_length() - 1
    copies = rep_count // 2
    exp_at = lax.axis_index("exp")
    rep_at = lax.axis_index("rep")
    width = tokens.shape[1]
    half = width // 2
    part = w_gate.shape[0]
    hidden = copies * part
    exp_peer = [{"exp": flipped(exp_at, d, exp_bits)} for d in range(exp_count)]
    x_peer = {"rep": flipped(rep_at, 1, rep_bits)}
    y_peer = [{"rep": flipped(rep_at, 2 * f, rep_bits)} for f in range(copies)]

    barrier = pltpu.get_barrier_semaphore()
    peers = exp_peer[1:] + [x_peer] + y_peer[1:]
    for peer in peers:
        pl.semaphore_signal(barrier, inc=1, device_id=peer, device_id_type=pl.DeviceIdType.MESH)
    order = [d for d in range(exp_count // 2, exp_count)] + [d for d in range(exp_count // 2)]
    for d in order:
        picked = dot(select[d, :, : tokens.shape[0]], tokens[...]) + dot(
            select[d, :, tokens.shape[0] :], grads[...]
        )
        send[d] = picked.astype(BF16)
    pl.semaphore_wait(barrier, len(peers))

    started = []

    def remote(src, dst, sems, at, peer):
        copy = pltpu.make_async_remote_copy(
            src_ref=src,
            dst_ref=dst,
            send_sem=sems.at[(0, *at)],
            recv_sem=sems.at[(1, *at)],
            device_id=peer,
            device_id_type=pl.DeviceIdType.MESH,
        )
        copy.start()
        started.append(copy)
        return copy

    z_in, y_in, x_in = {}, {}, {}
    matrices = (w_gate, w_up, w_down)
    for f in range(1, copies):
        for m in range(3):
            y_in[m, f] = remote(matrices[m], weights.at[m, f], y_sems, (m, f), y_peer[f])
    for d in order:
        if d:
            z_in[d] = remote(send.at[d], recv.at[0, d], z_sems, (d,), exp_peer[d])
    x_in[0] = remote(send.at[0], recv.at[1, 0], x_sems, (0,), x_peer)
    recv[0, 0] = send[0]
    for m in range(3):
        weights[m, 0] = matrices[m][...]
    for d in range(1, exp_count):
        z_in[d].wait_recv()
        x_in[d] = remote(recv.at[0, d], recv.at[1, d], x_sems, (d,), x_peer)
        if d == exp_count // 2 - 1:
            for copy in y_in.values():
                copy.wait_recv()

    ones = jnp.ones((16, hidden), BF16)
    pad = jnp.zeros((128 - cap, hidden), F32)
    xr_in, xp_in = {}, {}
    matrix = [weights.at[m] for m in range(3)]

    def whole(m):
        return matrix[m][...].reshape(hidden, width)

    def forward(step):
        pieces_t, pieces_g = [], []
        for d in (2 * step, 2 * step + 1):
            x_in[d].wait_recv()
            for side in (0, 1):
                block = recv[side, d].astype(F32)
                pieces_t.append(block[:cap])
                pieces_g.append(block[cap:])
        at = pl.ds(step * 4 * cap, 4 * cap)
        rows_s = jnp.concatenate(pieces_t, axis=0).astype(BF16)
        grads_s = jnp.concatenate(pieces_g, axis=0).astype(BF16)
        rows[at] = rows_s
        row_grads[at] = grads_s
        gate = dot(rows_s, whole(0), NT)
        up = dot(rows_s, whole(1), NT)
        back = dot(grads_s, whole(2), NT)
        sig = jax.nn.sigmoid(gate)
        act = gate * sig
        hid_s = act * up
        d_gate[at] = (back * up * sig * (1.0 + gate * (1.0 - sig))).astype(BF16)
        d_up[at] = (back * act).astype(BF16)
        hid[at] = hid_s.astype(BF16)
        product = hid_s * back
        for i in range(4):
            d, side = 2 * step + i // 2, i % 2
            mine = jnp.concatenate([product[i * cap : (i + 1) * cap], pad], axis=0).astype(BF16)
            total = dot(ones, mine, NT)
            if side:
                xp_send[d] = total.astype(BF16)
                xp_in[d] = remote(xp_send.at[d], xp_recv.at[d], xp_sems, (d,), x_peer)
            else:
                keep_prob[d] = total

    def backward(step):
        at = pl.ds(step * 4 * cap, 4 * cap)
        partial = dot(d_gate[at], whole(0)) + dot(d_up[at], whole(1))
        for i in range(4):
            d, side = 2 * step + i // 2, i % 2
            piece = partial[i * cap : (i + 1) * cap]
            folded = jnp.concatenate([piece[:, :half], piece[:, half:]], axis=0)
            if side:
                x_send[d] = folded.astype(BF16)
                xr_in[d] = remote(x_send.at[d], x_recv.at[d], xr_sems, (d,), x_peer)
            else:
                keep[d] = folded

    zr_in = []

    def give_back(d):
        xp_in[d].wait_recv()
        xr_in[d].wait_recv()
        total = (keep[d] + x_recv[d].astype(F32)).astype(BF16)
        total_prob = (keep_prob[d] + xp_recv[d].astype(F32)).astype(BF16)
        if d == 0:
            ret[0] = total
            ret_prob[0] = total_prob
        else:
            z_send[d] = total
            zp_send[d] = total_prob
            zr_in.append(remote(z_send.at[d], ret.at[d], zr_sems, (d,), exp_peer[d]))
            zr_in.append(remote(zp_send.at[d], ret_prob.at[d], zp_sems, (d,), exp_peer[d]))

    steps = exp_count // 2
    for step in range(steps):
        forward(step)
        if step < steps - 1:
            backward(step)

    g_in = []
    lefts = (d_gate, d_up, hid)
    rights = (rows, rows, row_grads)
    for m in range(3):
        for f in range(1, copies):
            product = dot(lefts[m][:, f * part : (f + 1) * part], rights[m][...], TN)
            grads_out[m, f] = product.astype(BF16)
            g_in.append(remote(grads_out.at[m, f], peer_grads.at[m, f - 1], g_sems, (m, f), y_peer[f]))
        if m == 0:
            backward(steps - 1)
            for d in range(exp_count // 2):
                give_back(d)
    for m in range(3):
        own_grads[m] = dot(lefts[m][:, :part], rights[m][...], TN)
        if m == 1:
            for d in range(exp_count // 2, exp_count):
                give_back(d)
    for copy in zr_in + g_in:
        copy.wait_recv()
    for copy in started:
        copy.wait_send()


def shards(rep_count, tokens, grad_out, expert_ids, probs, w_gate, w_up, w_down):
    count, width = tokens.shape
    exp_count = lax.axis_size("exp")
    copies = rep_count // 2
    part = w_gate.shape[1]
    hidden = copies * part
    cap = -(-(5 * count // (2 * exp_count)) // 8) * 8
    slots = exp_count * cap
    half = width // 2
    chosen = expert_ids.reshape(-1)
    pair = jnp.arange(2 * count, dtype=jnp.int32)
    same = (chosen[:, None] == chosen[None, :]) & (pair[None, :] < pair[:, None])
    ranks = jnp.sum(same.astype(jnp.int32), axis=1)
    slot_of = (chosen ^ lax.axis_index("exp")) * cap + ranks
    slot_pair = slot_of.reshape(count, 2)
    slot = jnp.arange(slots, dtype=jnp.int32)[:, None]
    hits = [slot_pair[:, k][None, :] == slot for k in (0, 1)]
    picks = (hits[0] | hits[1]).astype(BF16)
    scaled = jnp.where(hits[0], probs[:, 0][None, :], jnp.where(hits[1], probs[:, 1][None, :], 0))
    zero = jnp.zeros((exp_count, cap, count), BF16)
    select = jnp.concatenate(
        [
            jnp.concatenate([picks.reshape(exp_count, cap, count), zero], axis=2),
            jnp.concatenate([zero, scaled.astype(BF16).reshape(exp_count, cap, count)], axis=2),
        ],
        axis=1,
    )
    vmem = pl.BlockSpec(memory_space=pltpu.VMEM)
    total_rows = 2 * slots
    blocks = (exp_count, 2 * cap, half)
    dma = pltpu.SemaphoreType.DMA
    ret, ret_prob, own_grads, peer_grads = pl.pallas_call(
        functools.partial(layer, exp_count, rep_count, cap),
        out_shape=(
            jax.ShapeDtypeStruct(blocks, BF16),
            jax.ShapeDtypeStruct((exp_count, 16, 128), BF16),
            jax.ShapeDtypeStruct((3, part, width), F32),
            jax.ShapeDtypeStruct((3, copies - 1, part, width), BF16),
        ),
        in_specs=[vmem] * 6,
        out_specs=(vmem,) * 4,
        scratch_shapes=[
            pltpu.VMEM((exp_count, 2 * cap, width), BF16),
            pltpu.VMEM((2, exp_count, 2 * cap, width), BF16),
            pltpu.VMEM((3, copies, part, width), BF16),
            pltpu.VMEM((total_rows, width), BF16),
            pltpu.VMEM((total_rows, width), BF16),
            pltpu.VMEM((total_rows, hidden), BF16),
            pltpu.VMEM((total_rows, hidden), BF16),
            pltpu.VMEM((total_rows, hidden), BF16),
            pltpu.VMEM(blocks, BF16),
            pltpu.VMEM(blocks, BF16),
            pltpu.VMEM(blocks, F32),
            pltpu.VMEM(blocks, BF16),
            pltpu.VMEM((exp_count, 16, 128), BF16),
            pltpu.VMEM((exp_count, 16, 128), BF16),
            pltpu.VMEM((exp_count, 16, 128), F32),
            pltpu.VMEM((exp_count, 16, 128), BF16),
            pltpu.VMEM((3, copies, part, width), BF16),
            dma((2, exp_count)),
            dma((2, exp_count)),
            dma((2, 3, copies)),
            dma((2, exp_count)),
            dma((2, exp_count)),
            dma((2, exp_count)),
            dma((2, exp_count)),
            dma((2, 3, copies)),
        ],
        compiler_params=pltpu.CompilerParams(
            collective_id=0, has_side_effects=True, vmem_limit_bytes=56 * 1024 * 1024
        ),
        cost_estimate=pl.CostEstimate(
            flops=16 * total_rows * hidden * width, bytes_accessed=16 << 20, transcendentals=0
        ),
    )(select, tokens, grad_out, w_gate[0], w_up[0], w_down[0])
    back = [
        lax.dot_general(picks, ret[:, c * cap : (c + 1) * cap].reshape(slots, half), TN, preferred_element_type=F32)
        for c in (0, 1)
    ]
    grad_tokens = jnp.concatenate(back, axis=1).astype(BF16)
    prob_back = ret_prob[:, 0, :cap].reshape(slots, 1).astype(F32)
    grad_probs = jnp.stack(
        [jnp.sum(jnp.where(hit, prob_back, 0.0), axis=0) for hit in hits], axis=1
    ) / probs.astype(F32)
    full = own_grads + jnp.sum(peer_grads.astype(F32), axis=1)
    return (grad_tokens, grad_probs, full[0][None], full[1][None], full[2][None])


def solution(mesh):
    rows = P(("exp", "rep"), None)
    weight = P("exp", "rep", None)
    return jax.shard_map(
        functools.partial(shards, mesh.shape["rep"]),
        mesh=mesh,
        in_specs=(rows, rows, rows, rows, weight, weight, weight),
        out_specs=(rows, rows, weight, weight, weight),
        check_vma=False,
    )
```

```python
import functools

import jax
import jax.numpy as jnp
from jax import lax
from jax.experimental import pallas as pl
from jax.experimental.pallas import tpu as pltpu
from jax.sharding import PartitionSpec as P

F32 = jnp.float32
BF16 = jnp.bfloat16
NT = (((1,), (1,)), ((), ()))
TN = (((0,), (0,)), ((), ()))


def flipped(index, mask, bits):
    for bit in range(bits):
        if mask >> bit & 1:
            index = index + (1 << bit) - 2 * (1 << bit) * (index // (1 << bit) % 2)
    return index


def dot(a, b, dims=(((1,), (0,)), ((), ()))):
    return lax.dot_general(a, b, dims, preferred_element_type=F32)


def layer(
    exp_count,
    rep_count,
    cap,
    select,
    hits,
    tokens,
    grads,
    w_gate,
    w_up,
    w_down,
    grad_tokens,
    grad_probs,
    own_gate,
    own_up,
    own_down,
    peer_gate,
    peer_up,
    peer_down,
    send,
    recv,
    weights,
    rows,
    row_grads,
    own_units,
    rest_units,
    x_send,
    x_recv,
    keep,
    z_send,
    ret,
    xp_send,
    xp_recv,
    keep_prob,
    zp_send,
    ret_prob,
    grads_out,
    z_sems,
    x_sems,
    y_sems,
    xr_sems,
    zr_sems,
    xp_sems,
    zp_sems,
    g_sems,
):
    exp_bits = exp_count.bit_length() - 1
    rep_bits = rep_count.bit_length() - 1
    copies = rep_count // 2
    exp_at = lax.axis_index("exp")
    rep_at = lax.axis_index("rep")
    count, width = tokens.shape
    half = width // 2
    part = w_gate.shape[0]
    exp_peer = [{"exp": flipped(exp_at, d, exp_bits)} for d in range(exp_count)]
    x_peer = {"rep": flipped(rep_at, 1, rep_bits)}
    y_peer = [{"rep": flipped(rep_at, 2 * f, rep_bits)} for f in range(copies)]
    far = range(exp_count // 4, exp_count // 2)
    near = range(1, exp_count // 4)
    steps = [0, *far, *near]

    barrier = pltpu.get_barrier_semaphore()
    peers = exp_peer[1:] + [x_peer] + y_peer[1:]
    for peer in peers:
        pl.semaphore_signal(barrier, inc=1, device_id=peer, device_id_type=pl.DeviceIdType.MESH)

    def pick(d):
        picked = dot(select[d, :, :count], tokens[...]) + dot(select[d, :, count:], grads[...])
        send[d] = picked.astype(BF16)

    started = []

    def remote(src, dst, sems, at, peer):
        copy = pltpu.make_async_remote_copy(
            src_ref=src,
            dst_ref=dst,
            send_sem=sems.at[(0, *at)],
            recv_sem=sems.at[(1, *at)],
            device_id=peer,
            device_id_type=pl.DeviceIdType.MESH,
        )
        copy.start()
        started.append(copy)
        return copy

    z_in, y_in, x_in = {}, {}, {}
    matrices = (w_gate, w_up, w_down)
    pick(0)
    pick(1)
    pl.semaphore_wait(barrier, len(peers))
    z_in[1] = remote(send.at[1], recv.at[0, 1], z_sems, (1,), exp_peer[1])
    x_in[0] = remote(send.at[0], recv.at[1, 0], x_sems, (0,), x_peer)
    for f in range(1, copies):
        for m in range(3):
            y_in[m, f] = remote(matrices[m], weights.at[m, f], y_sems, (m, f), y_peer[f])
    for step in steps[1:]:
        for d in (2 * step, 2 * step + 1):
            pick(d)
            z_in[d] = remote(send.at[d], recv.at[0, d], z_sems, (d,), exp_peer[d])
    recv[0, 0] = send[0]
    for m in range(3):
        weights[m, 0] = matrices[m][...]

    ones = jnp.ones((16, part * (copies - 1)), BF16)

    def load(step):
        pieces_t, pieces_g = [], []
        for d in (2 * step, 2 * step + 1):
            x_in[d].wait_recv()
            for side in (0, 1):
                block = recv[side, d].astype(F32)
                pieces_t.append(block[:cap])
                pieces_g.append(block[cap:])
        at = pl.ds(step * 4 * cap, 4 * cap)
        rows[at] = jnp.concatenate(pieces_t, axis=0).astype(BF16)
        row_grads[at] = jnp.concatenate(pieces_g, axis=0).astype(BF16)

    def matrix(m, first, last):
        return weights[m, first:last].reshape((last - first) * part, width)

    def forward(step, first, last, units, fresh):
        at = pl.ds(step * 4 * cap, 4 * cap)
        gate = dot(rows[at], matrix(0, first, last), NT)
        up = dot(rows[at], matrix(1, first, last), NT)
        back = dot(row_grads[at], matrix(2, first, last), NT)
        sig = jax.nn.sigmoid(gate)
        act = gate * sig
        hid = act * up
        units[0, at] = (back * up * sig * (1.0 + gate * (1.0 - sig))).astype(BF16)
        units[1, at] = (back * act).astype(BF16)
        units[2, at] = hid.astype(BF16)
        product = hid * back
        wide = (last - first) * part
        pad = jnp.zeros((128 - cap, wide), F32)
        for i in range(4):
            d, side = 2 * step + i // 2, i % 2
            mine = jnp.concatenate([product[i * cap : (i + 1) * cap], pad], axis=0).astype(BF16)
            total = dot(ones[:, :wide], mine, NT)
            if fresh:
                keep_prob[side, d] = total
            else:
                keep_prob[side, d] += total

    def arrive(step):
        for d in (2 * step, 2 * step + 1):
            if d:
                z_in[d].wait_recv()
                x_in[d] = remote(recv.at[0, d], recv.at[1, d], x_sems, (d,), x_peer)

    def early(step):
        load(step)
        forward(step, 0, 1, own_units, True)

    for i, step in enumerate(steps):
        arrive(step)
        if i:
            early(steps[i - 1])
    for copy in y_in.values():
        copy.wait_recv()
    for step in steps[:-1]:
        forward(step, 1, copies, rest_units, False)
    load(steps[-1])
    forward(steps[-1], 1, copies, rest_units, True)

    g_in = []
    rights = (rows, rows, row_grads)
    own_grads = (own_gate, own_up, own_down)
    peer_grads = (peer_gate, peer_up, peer_down)
    for m in range(3):
        for f in range(1, copies):
            product = dot(rest_units[m, :, (f - 1) * part : f * part], rights[m][...], TN)
            grads_out[m, f] = product.astype(BF16)
            g_in.append(remote(grads_out.at[m, f], peer_grads[m].at[f - 1], g_sems, (m, f), y_peer[f]))
    forward(steps[-1], 0, 1, own_units, False)

    xr_in, xp_in = {}, {}

    def backward(step):
        at = pl.ds(step * 4 * cap, 4 * cap)
        partial = jnp.zeros((4 * cap, width), F32)
        for m in (0, 1):
            partial += dot(own_units[m, at], matrix(m, 0, 1))
            partial += dot(rest_units[m, at], matrix(m, 1, copies))
        for i in range(4):
            d, side = 2 * step + i // 2, i % 2
            piece = partial[i * cap : (i + 1) * cap]
            folded = jnp.concatenate([piece[:, :half], piece[:, half:]], axis=0)
            if side:
                x_send[d] = folded.astype(BF16)
                xp_send[d] = keep_prob[1, d].astype(BF16)
                xr_in[d] = remote(x_send.at[d], x_recv.at[d], xr_sems, (d,), x_peer)
                xp_in[d] = remote(xp_send.at[d], xp_recv.at[d], xp_sems, (d,), x_peer)
            else:
                keep[d] = folded

    zr_in = []

    def give_back(d):
        xp_in[d].wait_recv()
        xr_in[d].wait_recv()
        total = (keep[d] + x_recv[d].astype(F32)).astype(BF16)
        total_prob = (keep_prob[0, d] + xp_recv[d].astype(F32)).astype(BF16)
        if d == 0:
            ret[0] = total
            ret_prob[0] = total_prob
        else:
            z_send[d] = total
            zp_send[d] = total_prob
            zr_in.append(remote(z_send.at[d], ret.at[d], zr_sems, (d,), exp_peer[d]))
            zr_in.append(remote(zp_send.at[d], ret_prob.at[d], zp_sems, (d,), exp_peer[d]))

    back_steps = [*far, *near, 0]
    for step in back_steps:
        backward(step)
    for m, own in enumerate(own_grads):
        own[...] = dot(own_units[m], rights[m][...], TN)
        if m < 2:
            give_back(2 * back_steps[m])
            give_back(2 * back_steps[m] + 1)
    for step in back_steps[2:]:
        give_back(2 * step)
        give_back(2 * step + 1)
    for copy in zr_in:
        copy.wait_recv()
    picks = jnp.where(select[...].astype(F32) != 0.0, 1.0, 0.0).astype(BF16)
    blocks = exp_count * 2 * cap
    total = dot(picks.reshape(blocks, 2 * count), ret[...].reshape(blocks, half), TN)
    grad_tokens[:, :half] = total[:count].astype(BF16)
    grad_tokens[:, half:] = total[count:].astype(BF16)
    for k in (0, 1):
        probs_k = jnp.zeros((16, count), F32)
        for d in range(exp_count):
            probs_k += dot(ret_prob[d, :, :cap], hits[k, d])
        grad_probs[k] = probs_k
    for copy in g_in:
        copy.wait_recv()
    for copy in started:
        copy.wait_send()


def shards(rep_count, tokens, grad_out, expert_ids, probs, w_gate, w_up, w_down):
    count, width = tokens.shape
    exp_count = lax.axis_size("exp")
    copies = rep_count // 2
    part = w_gate.shape[1]
    hidden = copies * part
    cap = -(-(5 * count // (2 * exp_count)) // 8) * 8
    slots = exp_count * cap
    half = width // 2
    columns = expert_ids.T
    chosen = columns.reshape(-1)
    pair = jnp.arange(2 * count, dtype=jnp.int32)
    same = (chosen[:, None] == chosen[None, :]) & (pair[:, None] < pair[None, :])
    ranks = jnp.sum(same.astype(jnp.int32), axis=0)
    slot_pair = ((chosen ^ lax.axis_index("exp")) * cap + ranks).reshape(2, count)
    slot = jnp.arange(slots, dtype=jnp.int32)[:, None]
    found = [slot_pair[k][None, :] == slot for k in (0, 1)]
    hits = jnp.stack(found).astype(BF16).reshape(2, exp_count, cap, count)
    prob_pair = probs.T
    picks = (found[0] | found[1]).astype(BF16)
    scaled = jnp.where(found[0], prob_pair[0][None, :], jnp.where(found[1], prob_pair[1][None, :], 0))
    zero = jnp.zeros((exp_count, cap, count), BF16)
    select = jnp.concatenate(
        [
            jnp.concatenate([picks.reshape(exp_count, cap, count), zero], axis=2),
            jnp.concatenate([zero, scaled.astype(BF16).reshape(exp_count, cap, count)], axis=2),
        ],
        axis=1,
    )
    vmem = pl.BlockSpec(memory_space=pltpu.VMEM)
    total_rows = 2 * slots
    blocks = (exp_count, 2 * cap, half)
    prob_blocks = (exp_count, 16, 128)
    dma = pltpu.SemaphoreType.DMA
    grad_tokens, pair_probs, *parts = pl.pallas_call(
        functools.partial(layer, exp_count, rep_count, cap),
        out_shape=(
            jax.ShapeDtypeStruct((count, width), BF16),
            jax.ShapeDtypeStruct((2, 16, count), F32),
            *[jax.ShapeDtypeStruct((part, width), F32)] * 3,
            *[jax.ShapeDtypeStruct((copies - 1, part, width), BF16)] * 3,
        ),
        in_specs=[vmem] * 7,
        out_specs=(vmem,) * 8,
        scratch_shapes=[
            pltpu.VMEM((exp_count, 2 * cap, width), BF16),
            pltpu.VMEM((2, exp_count, 2 * cap, width), BF16),
            pltpu.VMEM((3, copies, part, width), BF16),
            pltpu.VMEM((total_rows, width), BF16),
            pltpu.VMEM((total_rows, width), BF16),
            pltpu.VMEM((3, total_rows, part), BF16),
            pltpu.VMEM((3, total_rows, hidden - part), BF16),
            pltpu.VMEM(blocks, BF16),
            pltpu.VMEM(blocks, BF16),
            pltpu.VMEM(blocks, F32),
            pltpu.VMEM(blocks, BF16),
            pltpu.VMEM(blocks, BF16),
            pltpu.VMEM(prob_blocks, BF16),
            pltpu.VMEM(prob_blocks, BF16),
            pltpu.VMEM((2, *prob_blocks), F32),
            pltpu.VMEM(prob_blocks, BF16),
            pltpu.VMEM(prob_blocks, BF16),
            pltpu.VMEM((3, copies, part, width), BF16),
            dma((2, exp_count)),
            dma((2, exp_count)),
            dma((2, 3, copies)),
            dma((2, exp_count)),
            dma((2, exp_count)),
            dma((2, exp_count)),
            dma((2, exp_count)),
            dma((2, 3, copies)),
        ],
        compiler_params=pltpu.CompilerParams(
            collective_id=0, has_side_effects=True, vmem_limit_bytes=56 * 1024 * 1024
        ),
        cost_estimate=pl.CostEstimate(
            flops=16 * total_rows * hidden * width, bytes_accessed=16 << 20, transcendentals=0
        ),
    )(select, hits, tokens, grad_out, w_gate[0], w_up[0], w_down[0])
    grad_probs = (pair_probs[:, 0, :] / prob_pair.astype(F32)).T
    full = [
        (own + jnp.sum(peer.astype(F32), axis=0))[None] for own, peer in zip(parts[:3], parts[3:])
    ]
    return (grad_tokens, grad_probs, *full)


def solution(mesh):
    rows = P(("exp", "rep"), None)
    weight = P("exp", "rep", None)
    return jax.shard_map(
        functools.partial(shards, mesh.shape["rep"]),
        mesh=mesh,
        in_specs=(rows, rows, rows, rows, weight, weight, weight),
        out_specs=(rows, rows, weight, weight, weight),
        check_vma=False,
    )
```
